256 devices in a mesh: dp: 16 (over x_hi, z), mp: 16 (over y, x_lo, core).
Axes of the slice: x: 4 (x_hi: 2, x_lo: 2; x = x_hi * 2 + x_lo), y: 4, z: 8, core: 2. Of those that a mesh axis runs over, the one named last changes fastest.
Arguments:
- out_grads: bfloat16 [4096, 8192], P('dp'), may hold values from -6 to 6
- hidden_acts: bfloat16 [4096, 28672], P('dp', 'mp'), may hold values from -6 to 6
- out_basis: bfloat16 [16, 512, 512], P('mp'), may hold values from -0.25 to 0.25
- in_basis: bfloat16 [112, 256, 256], P('mp'), may hold values from -0.375 to 0.375
- left_store: bfloat16 [16, 512, 8192], P('dp', None, 'mp'), may hold values from -0.0625 to 0.0625
- right_store: bfloat16 [16, 512, 28672], P('dp', None, 'mp'), may hold values from -0.03125 to 0.03125
- owners: int32 [16], replicated, may hold values from 0 to 15, as said below
Outputs:
- scores: float32 [32, 16], P('dp')
The draws below stay inside these ranges and needn't reach their ends.
Inputs may be any that keep to these rules, and one draw needn't show every extreme that they name: `owners`: every group index is the owner of exactly 16 // 16 queries.
All inputs are finite; a program needn't handle non-finite values.
Results may differ from the reference program's by a relative error of at most 0.0003.
Values may be sent and summed in bfloat16 or wider, within the bound.
A program may use at most 128 MiB of HBM per device.

```python
import jax
import jax.numpy as jnp
from jax import lax

D = 8192
FF = 28672
BS = 512
BA = 256
NQ = 16
R = 32
LEN = 128
TOKENS = 4096
N_DP = 16


def draw_owners(key, part):
    key = jax.random.fold_in(key, 7)
    shuffled = jax.random.permutation(key, N_DP).astype(jnp.int32)
    return jnp.tile(shuffled, NQ // N_DP)


def levels(key, dims, split, least, largest):
    factor_of = 1.0
    for axis_at, shards_of in split:
        draws = jax.random.uniform(jax.random.fold_in(jax.random.fold_in(key, 6), axis_at), (shards_of,), jnp.float32, least / len(split), largest / len(split))
        factor_of = factor_of * jnp.repeat(jnp.exp(draws), dims[axis_at] // shards_of).reshape((-1,) + (1,) * (len(dims) - 1 - axis_at))
    return factor_of


def noise(stream_key, dims, width, reach, cuts=(), kind=jnp.bfloat16):
    drawn = width * jax.random.normal(stream_key, dims, jnp.float32)
    if cuts:
        drawn = drawn * levels(stream_key, dims, cuts, -0.22, 0.18)
    return jnp.clip(drawn, -reach, reach).astype(kind)


def setup_inputs(seed: int = 0) -> dict:
    splits = jax.random.split(jax.random.key(seed), 8)
    out_grads = noise(splits[0], (TOKENS, D), 1.0, 6.0, ((0, 16),))
    hidden_acts = noise(splits[1], (TOKENS, FF), 1.0, 6.0, ((0, 16), (1, 16)))
    out_basis = noise(splits[2], (D // BS, BS, BS), BS ** -0.5, 0.25, ((0, 16),))
    in_basis = noise(splits[3], (FF // BA, BA, BA), BA ** -0.5, 0.375, ((0, 16),))
    left_store = noise(splits[4], (N_DP, NQ * R, D), D ** -0.5, 0.0625, ((0, 16), (2, 16)))
    right_store = noise(splits[5], (N_DP, NQ * R, FF), FF ** -0.5, 0.03125, ((0, 16), (2, 16)))
    owners = draw_owners(jax.random.fold_in(splits[7], 71), 0)
    return dict(out_grads=out_grads, hidden_acts=hidden_acts, out_basis=out_basis, in_basis=in_basis, left_store=left_store, right_store=right_store, owners=owners)


def pick_factors(factor_store, owners):
    columns = jnp.repeat(owners, R)
    chosen = columns[None, :] == jnp.arange(factor_store.shape[0], dtype=jnp.int32)[:, None]
    return jnp.sum(jnp.where(chosen[:, :, None], factor_store.astype(jnp.float32), jnp.float32(0.0)), axis=0)


def rotate(matrix_rows, eigenbasis, block_width):
    blocks = matrix_rows.astype(jnp.float32).reshape(matrix_rows.shape[0], -1, block_width)
    turned = jnp.einsum("tbi,bij->tbj", blocks, eigenbasis.astype(jnp.float32), precision=lax.Precision.HIGHEST)
    return turned.reshape(matrix_rows.shape[0], -1)


def reference(out_grads, hidden_acts, out_basis, in_basis, left_store, right_store, owners):
    left = pick_factors(left_store, owners)
    right = pick_factors(right_store, owners)

    def per_sequence(sequence_pair):
        grad_rows, act_rows = sequence_pair
        contract = (((1,), (1,)), ((), ()))
        coefficient = lax.dot_general(rotate(grad_rows, out_basis, BS), left, contract, precision=lax.Precision.HIGHEST)
        projected = lax.dot_general(rotate(act_rows, in_basis, BA), right, contract, precision=lax.Precision.HIGHEST)
        return jnp.sum((coefficient * projected).reshape(LEN, NQ, R), axis=(0, 2)) / jnp.float32(LEN)

    return lax.map(per_sequence, (out_grads.reshape(-1, LEN, D), hidden_acts.reshape(-1, LEN, FF)))
```

```python
import functools

import jax
import jax.numpy as jnp
from jax import lax
from jax.experimental import pallas as pl
from jax.experimental.pallas import tpu as pltpu
from jax.sharding import PartitionSpec as P

NQ = 16
R = 32
LEN = 128
TOK = 256
KL = 512
KA = 1024
KB = 768
BA = 256
MESH = pl.DeviceIdType.MESH
F32 = jnp.float32
BF16 = jnp.bfloat16

SLOTS = (
    (0, 0), (0, 1), (0, -1), (1, 0), (0, 2), (0, -2), (1, 1), (1, -1),
    (1, -2), (1, 2), (0, -3), (0, 3), (1, 3), (1, -3), (0, 4), (1, 4),
)
INDEX = {slot: i for i, slot in enumerate(SLOTS)}
HALF = 8 * R
CROSS = {"L": (0, 1, -1, 2, -2), "A": (0, 1, -1, 4), "B": (0, 1, -1, 2, -2)}
LAST_OWN = {"A": 1, "B": 1}
LAST_OTHER = {"A": 1, "B": -1}

ORDER = (
    ("L", 0, -1), ("L", 0, 1), ("L", 1, 0), ("L", 0, -2), ("L", 0, 2),
    ("A", 0, -1), ("A", 0, 1), ("A", 1, 0), ("B", 0, -1), ("B", 0, 1), ("B", 1, 0),
    ("L", 1, -1), ("L", 1, 1), ("coef", 0), ("L", 1, -2), ("L", 1, 2),
    ("L", 0, -3), ("L", 0, 3), ("L", 0, 4), ("core", 0), ("A", 0, 2), ("A", 0, -2), ("A", 1, -1),
    ("B", 0, 2), ("B", 0, -2), ("A", 1, 1), ("proj", 0), ("L", 1, 3), ("L", 1, -3), ("L", 1, 4),
    ("coef", 1), ("B", 1, -1), ("B", 1, 1), ("chips", 0), ("A", 0, -3), ("A", 0, 3), ("core", 1),
    ("B", 1, 2), ("A", 1, -2), ("B", 1, -2), ("A", 1, 2), ("B", 0, -3), ("B", 0, 3),
    ("proj", 1), ("A", 0, 4), ("spread", 0), ("proj", 2), ("B", 1, 3), ("A", 1, -3), ("chips", 1), ("A", 1, 3),
    ("B", 1, -3), ("B", 0, 4), ("B", 1, 4), ("A", 1, 4), ("proj", 3), ("spread", 1), ("sibling", 0), ("sibling", 1),
)


def wrap(d):
    return (d + 3) % 8 - 3


def routes(kind, o, d):
    out = []
    if kind == "L":
        if o == 0:
            if d == 0:
                out += [(1, 1), (-1, 1), (0, 0), (1, 2), (-1, 2)]
            if d == -2:
                out += [(1, 1), (1, 2)]
            if d == 2:
                out += [(-1, 1)]
            if d in (1, -1, 2, -2):
                out += [(0, 0)]
        else:
            if d == -2:
                out += [(1, 1)]
            if d == 2:
                out += [(-1, 1), (-1, 2)]
        return out
    if o == 0:
        if -2 <= d <= 0 or (d == -3 and LAST_OWN[kind] == 1):
            out.append((1, 1))
        if 0 <= d <= 2 or (d == 3 and LAST_OWN[kind] == -1):
            out.append((-1, 1))
        if d in CROSS[kind]:
            out.append((0, 0))
    else:
        if d <= 0:
            t = wrap(d - 1)
            if t not in CROSS[kind] and (t != 4 or LAST_OTHER[kind] == 1):
                out.append((1, 1))
        if 0 <= d < 4:
            t = d + 1
            if t not in CROSS[kind] and (t != 4 or LAST_OTHER[kind] == -1):
                out.append((-1, 1))
    return out


N_SENDS = sum(len(routes(k, o, d)) for k in "LAB" for o, d in SLOTS)
CHIPS = tuple((dy, a) for dy in range(4) for a in range(2) if (dy, a) != (0, 0))
PEERS = tuple((dy, a, e) for dy in range(4) for a in range(2) for e in range(2) if (dy, a, e) != (0, 0, 0))


def split(x):
    hi = x.astype(BF16)
    return hi, (x - hi.astype(F32)).astype(BF16)


def nt(a, b):
    return lax.dot_general(a, b, (((1,), (1,)), ((), ())), preferred_element_type=F32)


def kernel(owners, grads, acts, out_basis, in_basis, left_store, right_store, out,
           lst, rst, g, h, ob, ib, fl, fa, fb, rgh, rgl, rah, ral, pick,
           part, ain, summed, bin_, full, proj, tin,
           load_sem, gs, gr, as_, ar, bs, br, cs, cr, ds, dr, ts, tr):
    dp, mp = lax.axis_index("dp"), lax.axis_index("mp")
    xh, z = dp // 8, lax.rem(dp, 8)
    core = lax.rem(mp, 2)
    chip = mp // 2
    y, xl = chip // 2, lax.rem(chip, 2)

    def hop(direction, steps):
        if steps == 0:
            return ((1 - xh) * 8 + z, mp)
        return (xh * 8 + lax.rem(z + 8 + direction * steps, 8), mp)

    def chip_at(dy, a):
        return lax.rem(y + dy, 4) * 2 + (1 - xl if a else xl)

    def peer(dy, a, e):
        return (dp, chip_at(dy, a) * 2 + (1 - core if e else core))

    sibling = peer(0, 0, 1)

    loads = [
        pltpu.make_async_copy(left_store.at[0], lst, load_sem.at[0]),
        pltpu.make_async_copy(right_store.at[0], rst, load_sem.at[1]),
        pltpu.make_async_copy(grads.at[:, pl.ds(pl.multiple_of(mp * KL, KL), KL)], g, load_sem.at[2]),
        pltpu.make_async_copy(out_basis.at[0], ob, load_sem.at[3]),
        pltpu.make_async_copy(acts, h, load_sem.at[4]),
        pltpu.make_async_copy(in_basis, ib, load_sem.at[5]),
    ]
    for copy in loads:
        copy.start()

    barrier = pltpu.get_barrier_semaphore()
    greeted = [hop(1, 1), hop(-1, 1), hop(1, 2), hop(-1, 2), hop(0, 0)] + [peer(*p) for p in PEERS]
    for device in greeted:
        pl.semaphore_signal(barrier, inc=1, device_id=device, device_id_type=MESH)

    row = lax.broadcasted_iota(jnp.int32, (NQ, 128), 0)
    lane = lax.broadcasted_iota(jnp.int32, (NQ, 128), 1)
    group = jnp.zeros((NQ, 128), jnp.int32)
    for i, (o, d) in enumerate(SLOTS):
        ring = 1 - xh if o else xh
        group = jnp.where(row == i, ring * 8 + lax.rem(z + 8 + d, 8), group)
    table = jnp.zeros((NQ, 128), F32)
    for q in range(NQ):
        table = jnp.where((lane == q) & (group == owners[q]), jnp.float32(1), table)
    pick[...] = table

    chosen = []
    for q in range(NQ):
        owned = jnp.full((R, 128), owners[q], jnp.int32) == dp
        chosen.append(jnp.where(owned, jnp.float32(1), jnp.float32(0)).astype(BF16))

    def own_rows(store, first, width, dest):
        for left in range(0, width, 128):
            columns = slice(first + left, first + left + 128)
            total = chosen[0] * store[0:R, columns]
            for q in range(1, NQ):
                total = total + chosen[q] * store[q * R:(q + 1) * R, columns]
            dest[0:R, left:left + 128] = total

    loads[0].wait()
    own_rows(lst, 0, KL, fl)
    loads[1].wait()
    own_rows(rst, 0, KA, fa)
    own_rows(rst, KA, KB, fb)

    buffers = {"L": fl, "A": fa, "B": fb}
    sends = []

    def slot_ref(kind, o, d):
        return buffers[kind].at[pl.ds(INDEX[o, d] * R, R), :]

    def sem_of(kind, o, d):
        return gr.at["LAB".index(kind) * NQ + INDEX[o, d]]

    def forward(kind, o, d):
        for direction, steps in routes(kind, o, d):
            target = (1 - o, d) if steps == 0 else (o, wrap(d - direction * steps))
            copy = pltpu.make_async_remote_copy(
                src_ref=slot_ref(kind, o, d), dst_ref=slot_ref(kind, *target),
                send_sem=gs.at[len(sends)], recv_sem=sem_of(kind, *target),
                device_id=hop(direction, steps), device_id_type=MESH)
            copy.start()
            sends.append(copy)

    def take(kind, o, d):
        here = slot_ref(kind, o, d)
        pltpu.make_async_remote_copy(
            src_ref=here, dst_ref=here, send_sem=gs.at[0], recv_sem=sem_of(kind, o, d),
            device_id=sibling, device_id_type=MESH).wait_recv()
        forward(kind, o, d)

    pl.semaphore_wait(barrier, len(greeted))
    for kind in "LAB":
        forward(kind, 0, 0)

    loads[2].wait()
    loads[3].wait()
    hi, lo = split(jnp.dot(g[...], ob[...], preferred_element_type=F32))
    rgh[...] = hi
    rgl[...] = lo
    loads[4].wait()
    loads[5].wait()
    for c in range(7):
        columns = slice(c * BA, (c + 1) * BA)
        hi, lo = split(jnp.dot(h[:, columns], ib[c], preferred_element_type=F32))
        rah[:, columns] = hi
        ral[:, columns] = lo

    a_copies, b_copies, c_copies, d_copies = {}, {}, {}, {}
    my_half = pl.ds(pl.multiple_of(core * 128, 128), 128)
    its_half = pl.ds(pl.multiple_of((1 - core) * 128, 128), 128)

    def coef(b):
        x = fl[b * HALF:(b + 1) * HALF, :]
        part[b] = nt(x, rgh[...]) + nt(x, rgl[...])
        copy = pltpu.make_async_remote_copy(
            src_ref=part.at[b, its_half], dst_ref=ain.at[b], send_sem=as_.at[b], recv_sem=ar.at[b],
            device_id=sibling, device_id_type=MESH)
        copy.start()
        a_copies[b] = copy

    def core_sum(b):
        a_copies[b].wait_recv()
        summed[b] = part[b, my_half] + ain[b]
        b_copies[b] = []
        for k, (dy, a) in enumerate(CHIPS):
            there = chip_at(dy, a)
            copy = pltpu.make_async_remote_copy(
                src_ref=summed.at[b, pl.ds(pl.multiple_of(there * 16, 16), 16)], dst_ref=bin_.at[b, k],
                send_sem=bs.at[b, k], recv_sem=br.at[b, k], device_id=peer(dy, a, 0), device_id_type=MESH)
            copy.start()
            b_copies[b].append(copy)

    my_rows = pl.ds(pl.multiple_of(core * 128 + chip * 16, 16), 16)

    def chip_sum(b):
        total = summed[b, pl.ds(pl.multiple_of(chip * 16, 16), 16)]
        for k, copy in enumerate(b_copies[b]):
            copy.wait_recv()
            total = total + bin_[b, k]
        full[b, my_rows] = total
        c_copies[b] = []
        for k, (dy, a) in enumerate(CHIPS):
            copy = pltpu.make_async_remote_copy(
                src_ref=full.at[b, my_rows], dst_ref=full.at[b, my_rows],
                send_sem=cs.at[b, k], recv_sem=cr.at[b, k], device_id=peer(dy, a, 0), device_id_type=MESH)
            copy.start()
            c_copies[b].append(copy)

    def spread(b):
        for copy in c_copies[b]:
            copy.wait_recv()
        copy = pltpu.make_async_remote_copy(
            src_ref=full.at[b, my_half], dst_ref=full.at[b, my_half], send_sem=ds.at[b], recv_sem=dr.at[b],
            device_id=sibling, device_id_type=MESH)
        copy.start()
        d_copies[b] = copy

    def project(i):
        r = slice(i * 128, (i + 1) * 128)
        xa, xb = fa[r, :], fb[r, :]
        proj[r, :] = (nt(xa, rah[:, :KA]) + nt(xa, ral[:, :KA])) + (nt(xb, rah[:, KA:]) + nt(xb, ral[:, KA:]))

    for step in ORDER:
        if step[0] in buffers:
            take(*step)
        elif step[0] == "coef":
            coef(step[1])
        elif step[0] == "core":
            core_sum(step[1])
        elif step[0] == "chips":
            chip_sum(step[1])
        elif step[0] == "spread":
            spread(step[1])
        elif step[0] == "sibling":
            d_copies[step[1]].wait_recv()
        else:
            project(step[1])

    sums = []
    for b in range(2):
        both = full[b] * proj[b * HALF:(b + 1) * HALF, :]
        sums.append(jnp.sum(both.reshape(8, R, TOK), axis=1))
    per_slot = jnp.concatenate(sums, axis=0)
    table = pick[...]
    first = jnp.sum(jnp.sum(per_slot[:, :LEN], axis=1, keepdims=True) * table, axis=0, keepdims=True)
    second = jnp.sum(jnp.sum(per_slot[:, LEN:], axis=1, keepdims=True) * table, axis=0, keepdims=True)
    sub = lax.broadcasted_iota(jnp.int32, (8, 128), 0)
    tin[mp] = jnp.where(sub == 0, first, jnp.where(sub == 1, second, jnp.float32(0)))
    t_copies = []
    for k, p in enumerate(PEERS):
        copy = pltpu.make_async_remote_copy(
            src_ref=tin.at[mp], dst_ref=tin.at[mp], send_sem=ts.at[k], recv_sem=tr.at[k],
            device_id=peer(*p), device_id_type=MESH)
        copy.start()
        t_copies.append(copy)
    for copy in sends:
        copy.wait_send()
    for b in range(2):
        a_copies[b].wait_send()
        for copy in b_copies[b] + c_copies[b]:
            copy.wait_send()
        d_copies[b].wait_send()
    for copy in t_copies:
        copy.wait()
    total = tin[0]
    for i in range(1, 16):
        total = total + tin[i]
    out[...] = total[:2, :NQ] * jnp.float32(1.0 / LEN)


def on_device(out_grads, hidden_acts, out_basis, in_basis, left_store, right_store, owners):
    n_chips, n_peers = len(CHIPS), len(PEERS)
    dma = pltpu.SemaphoreType.DMA
    return pl.pallas_call(
        kernel,
        out_shape=jax.ShapeDtypeStruct((2, NQ), F32),
        in_specs=[pl.BlockSpec(memory_space=pltpu.SMEM)] + [pl.BlockSpec(memory_space=pl.ANY)] * 6,
        out_specs=pl.BlockSpec(memory_space=pltpu.VMEM),
        scratch_shapes=[
            pltpu.VMEM((NQ * R, KL), BF16),
            pltpu.VMEM((NQ * R, KA + KB), BF16),
            pltpu.VMEM((TOK, KL), BF16),
            pltpu.VMEM((TOK, KA + KB), BF16),
            pltpu.VMEM((KL, KL), BF16),
            pltpu.VMEM((7, BA, BA), BF16),
            pltpu.VMEM((NQ * R, KL), BF16),
            pltpu.VMEM((NQ * R, KA), BF16),
            pltpu.VMEM((NQ * R, KB), BF16),
            pltpu.VMEM((TOK, KL), BF16),
            pltpu.VMEM((TOK, KL), BF16),
            pltpu.VMEM((TOK, KA + KB), BF16),
            pltpu.VMEM((TOK, KA + KB), BF16),
            pltpu.VMEM((NQ, 128), F32),
            pltpu.VMEM((2, HALF, TOK), F32),
            pltpu.VMEM((2, 128, TOK), F32),
            pltpu.VMEM((2, 128, TOK), F32),
            pltpu.VMEM((2, n_chips, 16, TOK), F32),
            pltpu.VMEM((2, HALF, TOK), F32),
            pltpu.VMEM((2 * HALF, TOK), F32),
            pltpu.VMEM((16, 8, 128), F32),
            dma((6,)), dma((N_SENDS,)), dma((3 * NQ,)),
            dma((2,)), dma((2,)), dma((2, n_chips)), dma((2, n_chips)), dma((2, n_chips)), dma((2, n_chips)),
            dma((2,)), dma((2,)), dma((n_peers,)), dma((n_peers,)),
        ],
        compiler_params=pltpu.CompilerParams(
            collective_id=0, has_side_effects=True, vmem_limit_bytes=48 * 2 ** 20),
    )(owners, out_grads, hidden_acts, out_basis, in_basis, left_store, right_store)


def solution(mesh):
    in_specs = (
        P("dp", None),
        P("dp", "mp"),
        P("mp", None, None),
        P("mp", None, None),
        P("dp", None, "mp"),
        P("dp", None, "mp"),
        P(),
    )
    return jax.shard_map(on_device, mesh=mesh, in_specs=in_specs, out_specs=P("dp", None), check_vma=False)
```

```python
import functools

import jax
import jax.numpy as jnp
from jax import lax
from jax.experimental import pallas as pl
from jax.experimental.pallas import tpu as pltpu
from jax.sharding import PartitionSpec as P

NQ = 16
R = 32
LEN = 128
TOK = 256
KL = 512
KA = 1024
KB = 768
BA = 256
MESH = pl.DeviceIdType.MESH
F32 = jnp.float32
BF16 = jnp.bfloat16

SLOTS = (
    (0, 0), (0, 1), (0, -1), (0, 2), (0, -2), (0, 3), (0, -3), (0, 4),
    (1, 0), (1, 1), (1, -1), (1, 2), (1, -2), (1, 3), (1, -3), (1, 4),
)
INDEX = {slot: i for i, slot in enumerate(SLOTS)}
BATCHES = ((0, 8, True), (8, 12, False), (12, 16, False))
LEFT_ROUTES = {
    (0, 0): ((0, 0), (1, 1), (-1, 1), (1, 2), (-1, 2),),
    (0, 1): ((0, 0),),
    (0, -1): ((0, 0),),
    (0, 2): ((-1, 1), (0, 0),),
    (0, -2): ((1, 1), (1, 2), (0, 0),),
    (1, 2): ((-1, 1), (-1, 2),),
    (1, -2): ((1, 1),),
}
CROSS = {"A": (0, 1, -1, 4), "B": (0, 1, -1, 2, -2)}
LAST_OWN = {"A": 1, "B": 1}
LAST_OTHER = {"A": 1, "B": -1}

ORDER = (
    ("L", 0, 1), ("L", 1, 0), ("L", 0, 2), ("A", 1, 0), ("A", 0, 1), ("B", 1, 0), ("B", 0, 1), ("L", 0, 3),
    ("L", 1, 1), ("L", 0, 4), ("coef", 0), ("L", 1, 2), ("coef", 1), ("A", 0, 2), ("B", 0, 2), ("proj", 0, 4),
    ("A", 1, 1), ("core", 0), ("L", 1, 3), ("A", 0, 3), ("L", 1, 4), ("B", 1, 1), ("coef", 2), ("B", 1, 2),
    ("B", 0, 3), ("reduce", 1), ("A", 1, 2), ("proj", 8, 12), ("A", 0, 4), ("reduce", 0), ("A", 1, 3), ("B", 1, 3),
    ("reduce", 2), ("B", 0, 4), ("proj", 4, 8), ("B", 1, 4), ("A", 1, 4), ("proj", 12, 16), ("whole", 1),
    ("whole", 0), ("halves", 0), ("whole", 2),
)


def wrap(d):
    return (d + 3) % 8 - 3


def routes(kind, o, d):
    if kind == "L":
        return LEFT_ROUTES.get((o, d), ())
    out = []
    if o == 0:
        if -2 <= d <= 0 or (d == -3 and LAST_OWN[kind] == 1):
            out.append((1, 1))
        if 0 <= d <= 2 or (d == 3 and LAST_OWN[kind] == -1):
            out.append((-1, 1))
        if d in CROSS[kind]:
            out.append((0, 0))
    else:
        if d <= 0:
            t = wrap(d - 1)
            if t not in CROSS[kind] and (t != 4 or LAST_OTHER[kind] == 1):
                out.append((1, 1))
        if 0 <= d < 4:
            t = d + 1
            if t not in CROSS[kind] and (t != 4 or LAST_OTHER[kind] == -1):
                out.append((-1, 1))
    return out


CHIPS = tuple((dy, a) for dy in (2, 1, 3, 0) for a in (1, 0) if (dy, a) != (0, 0))
PEERS = tuple((dy, a, e) for dy in (2, 1, 3, 0) for a in (1, 0) for e in (1, 0) if (dy, a, e) != (0, 0, 0))


def split(x):
    hi = x.astype(BF16)
    return hi, (x - hi.astype(F32)).astype(BF16)


def nt(a, b):
    return lax.dot_general(a, b, (((1,), (1,)), ((), ())), preferred_element_type=F32)


def kernel(owners, grads, acts, out_basis, in_basis, left_store, right_store, out,
           lst, rst, g, h, ob, ib, fl, fa, fb, rgh, rgl, rah, ral, pick,
           part, ain, summed, bin_, full, proj, tin,
           load_sem, out_sem, in_sem, mp_out, mp_in):
    dp, mp = lax.axis_index("dp"), lax.axis_index("mp")
    xh, z = dp // 8, lax.rem(dp, 8)
    core = lax.rem(mp, 2)
    chip = mp // 2
    y, xl = chip // 2, lax.rem(chip, 2)

    def hop(direction, steps):
        if steps == 0:
            return ((1 - xh) * 8 + z, mp)
        return (xh * 8 + lax.rem(z + 8 + direction * steps, 8), mp)

    def chip_at(dy, a):
        return lax.rem(y + dy, 4) * 2 + (1 - xl if a else xl)

    def peer(dy, a, e):
        return (dp, chip_at(dy, a) * 2 + (1 - core if e else core))

    sibling = peer(0, 0, 1)

    def steps_from(chip_index):
        return lax.rem(y + 4 - chip_index // 2, 4), lax.rem(xl + chip_index, 2)

    def chip_place(n):
        dy, a = steps_from(n)
        return dy * 2 + a

    def place(n):
        return chip_place(n // 2) * 2 + lax.rem(core + n, 2)

    barrier = pltpu.get_barrier_semaphore()
    greeted = [hop(1, 1), hop(-1, 1), hop(-1, 2), hop(1, 2), hop(0, 0)] + [peer(*p) for p in PEERS]
    for device in greeted:
        pl.semaphore_signal(barrier, inc=1, device_id=device, device_id_type=MESH)

    loads = [
        pltpu.make_async_copy(left_store.at[0], lst, load_sem.at[0]),
        pltpu.make_async_copy(right_store.at[0], rst, load_sem.at[1]),
        pltpu.make_async_copy(grads.at[:, pl.ds(pl.multiple_of(mp * KL, KL), KL)], g, load_sem.at[2]),
        pltpu.make_async_copy(out_basis.at[0], ob, load_sem.at[3]),
        pltpu.make_async_copy(acts, h, load_sem.at[4]),
        pltpu.make_async_copy(in_basis, ib, load_sem.at[5]),
    ]
    for copy in loads:
        copy.start()

    row = lax.broadcasted_iota(jnp.int32, (NQ, 128), 0)
    lane = lax.broadcasted_iota(jnp.int32, (NQ, 128), 1)
    group = jnp.zeros((NQ, 128), jnp.int32)
    for i, (o, d) in enumerate(SLOTS):
        ring = 1 - xh if o else xh
        group = jnp.where(row == i, ring * 8 + lax.rem(z + 8 + d, 8), group)
    table = jnp.zeros((NQ, 128), F32)
    for q in range(NQ):
        table = jnp.where((lane == q) & (group == owners[q]), jnp.float32(1), table)
    pick[...] = table

    chosen = []
    for q in range(NQ):
        owned = jnp.full((R, 128), owners[q], jnp.int32) == dp
        chosen.append(jnp.where(owned, jnp.float32(1), jnp.float32(0)).astype(BF16))

    def own_rows(store, first, width, dest):
        for left in range(0, width, 128):
            columns = slice(first + left, first + left + 128)
            total = chosen[0] * store[0:R, columns]
            for q in range(1, NQ):
                total = total + chosen[q] * store[q * R:(q + 1) * R, columns]
            dest[0:R, left:left + 128] = total

    def send(src, dst, send_sem, recv_sem, device):
        pltpu.make_async_remote_copy(
            src_ref=src, dst_ref=dst, send_sem=send_sem, recv_sem=recv_sem, device_id=device, device_id_type=MESH).start()

    def waiter(ref, send_sem, recv_sem):
        return pltpu.make_async_remote_copy(
            src_ref=ref, dst_ref=ref, send_sem=send_sem, recv_sem=recv_sem, device_id=sibling, device_id_type=MESH)

    def drain(ref, sem):
        waiter(ref, out_sem.at[0], sem).wait_recv()

    def drain_sent(ref, sem):
        waiter(ref, sem, in_sem.at[0]).wait_send()

    buffers = {"L": fl, "A": fa, "B": fb}

    def slot_ref(kind, o, d):
        return buffers[kind].at[pl.ds(INDEX[o, d] * R, R), :]

    def sem_of(kind, o, d):
        return in_sem.at["LAB".index(kind) * 9 + o * 5 + abs(d) - 1]

    def forward(kind, o, d):
        for direction, steps in routes(kind, o, d):
            target = (1 - o, d) if steps == 0 else (o, wrap(d - direction * steps))
            send(slot_ref(kind, o, d), slot_ref(kind, *target), out_sem.at["LAB".index(kind)], sem_of(kind, *target),
                 hop(direction, steps))

    def take(kind, o, d):
        pair = (d, -d) if 0 < d < 4 else (d,)
        drain(buffers[kind].at[pl.ds(INDEX[o, d] * R, len(pair) * R), :], sem_of(kind, o, d))
        for each in pair:
            forward(kind, o, each)

    loads[0].wait()
    own_rows(lst, 0, KL, fl)
    pl.semaphore_wait(barrier, len(greeted))
    forward("L", 0, 0)
    loads[1].wait()
    own_rows(rst, 0, KA, fa)
    forward("A", 0, 0)
    own_rows(rst, KA, KB, fb)
    forward("B", 0, 0)

    loads[2].wait()
    loads[3].wait()
    hi, lo = split(jnp.dot(g[...], ob[...], preferred_element_type=F32))
    rgh[...] = hi
    rgl[...] = lo
    loads[4].wait()
    loads[5].wait()
    for c in range(7):
        columns = slice(c * BA, (c + 1) * BA)
        hi, lo = split(jnp.dot(h[:, columns], ib[c], preferred_element_type=F32))
        rah[:, columns] = hi
        ral[:, columns] = lo

    my_half = pl.multiple_of(core * 128, 128)
    its_half = pl.multiple_of((1 - core) * 128, 128)
    sent = [0, 0, 0, 0]

    def piece(b, n):
        first, last, _ = BATCHES[b]
        size = (last - first) * R // 16
        return pl.ds(pl.multiple_of(first * R + n * size, size), size)

    def send_mp(b, stage, src, dst, device):
        sent[stage] += src.shape[0]
        send(src, dst, mp_out.at[stage], mp_in.at[b, stage], device)

    def others(b):
        if BATCHES[b][2]:
            return [(chip_at(*p), peer(*p, 0)) for p in CHIPS]
        return [(chip_at(dy, a) * 2 + (1 - core if e else core), peer(dy, a, e)) for dy, a, e in PEERS]

    def size_of(b):
        return (BATCHES[b][1] - BATCHES[b][0]) * R // 16

    def coef(b):
        first, last, staged = BATCHES[b]
        x = fl[first * R:last * R, :]
        part[first * R:last * R, :] = nt(x, rgh[...]) + nt(x, rgl[...])
        if staged:
            send_mp(b, 0, part.at[pl.ds(first * R + its_half, 128)], ain.at[b], sibling)
        else:
            for k, (n, device) in enumerate(others(b)):
                send_mp(b, 1, part.at[piece(b, n)], bin_.at[b, pl.ds(k * size_of(b), size_of(b))], device)

    def core_sum(b):
        drain(ain.at[b], mp_in.at[b, 0])
        summed[b] = part[pl.ds(BATCHES[b][0] * R + my_half, 128)] + ain[b]
        for k, (n, device) in enumerate(others(b)):
            send_mp(b, 1, summed.at[b, pl.ds(pl.multiple_of(n * 16, 16), 16)], bin_.at[b, pl.ds(k * 16, 16)], device)

    def reduce(b):
        staged, size = BATCHES[b][2], size_of(b)
        n = 7 if staged else 15
        drain(bin_.at[b, pl.ds(0, n * size)], mp_in.at[b, 1])
        total = summed[b, pl.ds(pl.multiple_of(chip * 16, 16), 16)] if staged else part[piece(b, mp), :]
        for k in range(n):
            total = total + bin_[b, k * size:(k + 1) * size]
        half = my_half if staged else 0
        full[b, pl.ds(half, size)] = total
        for k, (_, device) in enumerate(others(b)):
            at = (lambda dy, a: dy * 2 + a)(*CHIPS[k]) if staged else (lambda dy, a, e: dy * 4 + a * 2 + e)(*PEERS[k])
            send_mp(b, 2, full.at[b, pl.ds(half, size)], full.at[b, pl.ds(half + at * size, size)], device)

    def whole(b):
        staged, size = BATCHES[b][2], size_of(b)
        half, n = (my_half, 7) if staged else (0, 15)
        drain(full.at[b, pl.ds(half + size, n * size)], mp_in.at[b, 2])
        if staged:
            rows = pl.ds(my_half, 128)
            send_mp(b, 3, full.at[b, rows], full.at[b, rows], sibling)

    def halves(b):
        drain(full.at[b, pl.ds(its_half, 128)], mp_in.at[b, 3])

    def project(first, last):
        r = slice(first * R, last * R)
        xa, xb = fa[r, :], fb[r, :]
        proj[r, :] = (nt(xa, rah[:, :KA]) + nt(xa, ral[:, :KA])) + (nt(xb, rah[:, KA:]) + nt(xb, ral[:, KA:]))

    steps = {"coef": coef, "core": core_sum, "reduce": reduce, "whole": whole, "halves": halves, "proj": project}
    for step in ORDER:
        if step[0] in buffers:
            take(*step)
        else:
            steps[step[0]](*step[1:])

    slot_sums = []
    for b, (first, last, staged) in enumerate(BATCHES):
        size = size_of(b)
        per = R // size
        for i in range(last - first):
            total = jnp.zeros((size, TOK), F32)
            for n in range(i * per, (i + 1) * per):
                at = (n // 8) * 128 + chip_place(n % 8) * 16 if staged else place(n) * size
                total = total + (full[b, pl.ds(pl.multiple_of(at, size), size)]
                                 * proj[first * R + n * size:first * R + (n + 1) * size, :])
            slot_sums.append(jnp.sum(total, axis=0, keepdims=True))
    per_slot = jnp.concatenate(slot_sums, axis=0)
    table = pick[...]
    first = jnp.sum(jnp.sum(per_slot[:, :LEN], axis=1, keepdims=True) * table, axis=0, keepdims=True)
    second = jnp.sum(jnp.sum(per_slot[:, LEN:], axis=1, keepdims=True) * table, axis=0, keepdims=True)
    sub = lax.broadcasted_iota(jnp.int32, (8, 128), 0)
    tin[0] = jnp.where(sub == 0, first, jnp.where(sub == 1, second, jnp.float32(0)))
    for dy, a, e in PEERS:
        send(tin.at[0], tin.at[dy * 4 + a * 2 + e], mp_out.at[4], mp_in.at[0, 4], peer(dy, a, e))
    for kind in range(3):
        drain_sent((fl, fa, fb)[kind].at[pl.ds(0, 15 * R)], out_sem.at[kind])
    for stage in range(4):
        if sent[stage]:
            drain_sent(part.at[pl.ds(0, sent[stage])], mp_out.at[stage])
    drain_sent(tin.at[pl.ds(0, 15)], mp_out.at[4])
    drain(tin.at[pl.ds(1, 15)], mp_in.at[0, 4])
    total = tin[place(0)]
    for i in range(1, 16):
        total = total + tin[place(i)]
    out[...] = total[:2, :NQ] * jnp.float32(1.0 / LEN)


def on_device(out_grads, hidden_acts, out_basis, in_basis, left_store, right_store, owners):
    n_batches = len(BATCHES)
    dma = pltpu.SemaphoreType.DMA
    return pl.pallas_call(
        kernel,
        out_shape=jax.ShapeDtypeStruct((2, NQ), F32),
        in_specs=[pl.BlockSpec(memory_space=pltpu.SMEM)] + [pl.BlockSpec(memory_space=pltpu.HBM)] * 6,
        out_specs=pl.BlockSpec(memory_space=pltpu.VMEM),
        scratch_shapes=[
            pltpu.VMEM((NQ * R, KL), BF16),
            pltpu.VMEM((NQ * R, KA + KB), BF16),
            pltpu.VMEM((TOK, KL), BF16),
            pltpu.VMEM((TOK, KA + KB), BF16),
            pltpu.VMEM((KL, KL), BF16),
            pltpu.VMEM((7, BA, BA), BF16),
            pltpu.VMEM((NQ * R, KL), BF16),
            pltpu.VMEM((NQ * R, KA), BF16),
            pltpu.VMEM((NQ * R, KB), BF16),
            pltpu.VMEM((TOK, KL), BF16),
            pltpu.VMEM((TOK, KL), BF16),
            pltpu.VMEM((TOK, KA + KB), BF16),
            pltpu.VMEM((TOK, KA + KB), BF16),
            pltpu.VMEM((NQ, 128), F32),
            pltpu.VMEM((NQ * R, TOK), F32),
            pltpu.VMEM((n_batches, 128, TOK), F32),
            pltpu.VMEM((n_batches, 128, TOK), F32),
            pltpu.VMEM((n_batches, 120, TOK), F32),
            pltpu.VMEM((n_batches, NQ * R, TOK), F32),
            pltpu.VMEM((NQ * R, TOK), F32),
            pltpu.VMEM((16, 8, 128), F32),
            dma((6,)), dma((3,)), dma((27,)), dma((5,)), dma((n_batches, 5)),
        ],
        compiler_params=pltpu.CompilerParams(
            collective_id=0, has_side_effects=True, vmem_limit_bytes=62 * 2 ** 20),
    )(owners, out_grads, hidden_acts, out_basis, in_basis, left_store, right_store)


def solution(mesh):
    in_specs = (
        P("dp", None),
        P("dp", "mp"),
        P("mp", None, None),
        P("mp", None, None),
        P("dp", None, "mp"),
        P("dp", None, "mp"),
        P(),
    )
    return jax.shard_map(on_device, mesh=mesh, in_specs=in_specs, out_specs=P("dp", None), check_vma=False)
```

```python
import functools

import jax
import jax.numpy as jnp
from jax import lax
from jax.experimental import pallas as pl
from jax.experimental.pallas import tpu as pltpu
from jax.sharding import PartitionSpec as P

NQ = 16
R = 32
LEN = 128
TOK = 256
KL = 512
KR = 1792
BA = 256
KINDS = "LAB"
MESH = pl.DeviceIdType.MESH
F32 = jnp.float32
BF16 = jnp.bfloat16

SLOTS = (
    (0, 0), (0, 1), (0, -1), (0, 2), (0, -2), (0, 3), (0, -3), (0, 4),
    (1, 0), (1, 1), (1, -1), (1, 2), (1, -2), (1, 3), (1, -3), (1, 4),
)
INDEX = {slot: i for i, slot in enumerate(SLOTS)}
BATCHES = ((0, 8, True), (8, 12, False), (12, 16, False))
COLUMNS = {"A": (0, 1024), "B": (1024, 1792)}
LEFT_ROUTES = {
    (0, 0): ((0, 0), (1, 1), (-1, 1), (1, 2), (-1, 2),),
    (0, 1): ((0, 0),),
    (0, -1): ((0, 0),),
    (0, 2): ((-1, 1), (0, 0),),
    (0, -2): ((1, 1), (1, 2), (0, 0),),
    (1, 2): ((-1, 1), (-1, 2),),
    (1, -2): ((1, 1),),
}
CROSS = {"A": (0, 1, -1, 4), "B": (0, 1, -1, 2, -2)}
LAST_OWN = {"A": 1, "B": -1}
LAST_OTHER = {"A": 1, "B": -1}

ORDER = (
    ("L", 0, 1), ("L", 1, 0), ("L", 0, 2), ("A", 1, 0), ("A", 0, 1), ("B", 1, 0), ("B", 0, 1), ("L", 0, 3),
    ("L", 1, 1), ("L", 0, 4), ("coef", 0), ("L", 1, 2), ("coef", 1), ("A", 0, 2), ("core", 0), ("B", 0, 2),
    ("proj", 0, 4), ("A", 1, 1), ("L", 1, 3), ("L", 1, 4), ("coef", 2), ("A", 0, 3), ("B", 1, 1), ("reduce", 1),
    ("B", 0, 3), ("reduce", 0), ("B", 1, 2), ("A", 1, 2), ("proj", 8, 12), ("A", 0, 4), ("reduce", 2), ("B", 0, 4),
    ("proj", 4, 8), ("B", 1, 3), ("whole", 1), ("A", 1, 3), ("whole", 0), ("A", 1, 4), ("B", 1, 4), ("proj", 12, 16),
    ("halves", 0), ("whole", 2),
)


def wrap(d):
    return (d + 3) % 8 - 3


def routes(kind, o, d):
    if kind == "L":
        return LEFT_ROUTES.get((o, d), ())
    out = []
    if o == 0:
        if -2 <= d <= 0 or (d == -3 and LAST_OWN[kind] == 1):
            out.append((1, 1))
        if 0 <= d <= 2 or (d == 3 and LAST_OWN[kind] == -1):
            out.append((-1, 1))
        if d in CROSS[kind]:
            out.append((0, 0))
    else:
        if d <= 0:
            t = wrap(d - 1)
            if t not in CROSS[kind] and (t != 4 or LAST_OTHER[kind] == 1):
                out.append((1, 1))
        if 0 <= d < 4:
            t = d + 1
            if t not in CROSS[kind] and (t != 4 or LAST_OTHER[kind] == -1):
                out.append((-1, 1))
    return out


CHIPS = tuple((dy, a) for dy in (2, 1, 3, 0) for a in (1, 0) if (dy, a) != (0, 0))
PEERS = tuple((dy, a, e) for dy in (2, 1, 3, 0) for a in (1, 0) for e in (1, 0) if (dy, a, e) != (0, 0, 0))


def split(x):
    hi = x.astype(BF16)
    return hi, (x - hi.astype(F32)).astype(BF16)


def turned(basis, rows):
    return lax.dot_general(basis, rows, (((0,), (1,)), ((), ())), preferred_element_type=F32)


def mm(a, b):
    return jnp.dot(a, b, preferred_element_type=F32)


def kernel(owners, grads, acts, out_basis, in_basis, left_store, right_store, out,
           lst, rst, g, h, ob, ib, fl, fa, fb, rgh, rgl, rah, ral, pick,
           part, ain, summed, bin_, full, proj, tin,
           load_sem, out_sem, in_sem, mp_out, mp_in):
    dp, mp = lax.axis_index("dp"), lax.axis_index("mp")
    xh, z = dp // 8, lax.rem(dp, 8)
    core = lax.rem(mp, 2)
    chip = mp // 2
    y, xl = chip // 2, lax.rem(chip, 2)

    def hop(direction, steps):
        if steps == 0:
            return ((1 - xh) * 8 + z, mp)
        return (xh * 8 + lax.rem(z + 8 + direction * steps, 8), mp)

    def chip_at(dy, a):
        return lax.rem(y + dy, 4) * 2 + (1 - xl if a else xl)

    def peer(dy, a, e):
        return (dp, chip_at(dy, a) * 2 + (1 - core if e else core))

    sibling = peer(0, 0, 1)

    def steps_from(chip_index):
        return lax.rem(y + 4 - chip_index // 2, 4), lax.rem(xl + chip_index, 2)

    def chip_place(n):
        dy, a = steps_from(n)
        return dy * 2 + a

    def place(n):
        return chip_place(n // 2) * 2 + lax.rem(core + n, 2)

    barrier = pltpu.get_barrier_semaphore()
    greeted = [hop(1, 1), hop(-1, 1), hop(-1, 2), hop(1, 2), hop(0, 0)] + [peer(*p) for p in PEERS]
    for device in greeted:
        pl.semaphore_signal(barrier, inc=1, device_id=device, device_id_type=MESH)

    loads = [
        pltpu.make_async_copy(left_store.at[0], lst, load_sem.at[0]),
        pltpu.make_async_copy(right_store.at[0], rst, load_sem.at[1]),
        pltpu.make_async_copy(grads.at[:, pl.ds(pl.multiple_of(mp * KL, KL), KL)], g, load_sem.at[2]),
        pltpu.make_async_copy(out_basis.at[0], ob, load_sem.at[3]),
        pltpu.make_async_copy(acts, h, load_sem.at[4]),
        pltpu.make_async_copy(in_basis, ib, load_sem.at[5]),
    ]
    for copy in loads:
        copy.start()

    row = lax.broadcasted_iota(jnp.int32, (NQ, 128), 0)
    lane = lax.broadcasted_iota(jnp.int32, (NQ, 128), 1)
    group = jnp.zeros((NQ, 128), jnp.int32)
    for i, (o, d) in enumerate(SLOTS):
        ring = 1 - xh if o else xh
        group = jnp.where(row == i, ring * 8 + lax.rem(z + 8 + d, 8), group)
    table = jnp.zeros((NQ, 128), F32)
    for q in range(NQ):
        table = jnp.where((lane == q) & (group == owners[q]), jnp.float32(1), table)
    pick[...] = table

    chosen = []
    for q in range(NQ):
        owned = jnp.full((R, 128), owners[q], jnp.int32) == dp
        chosen.append(jnp.where(owned, jnp.float32(1), jnp.float32(0)).astype(BF16))

    def own_rows(store, first, width, dest):
        for left in range(0, width, 128):
            columns = slice(first + left, first + left + 128)
            total = chosen[0] * store[0:R, columns]
            for q in range(1, NQ):
                total = total + chosen[q] * store[q * R:(q + 1) * R, columns]
            dest[0:R, left:left + 128] = total

    def send(src, dst, send_sem, recv_sem, device):
        pltpu.make_async_remote_copy(
            src_ref=src, dst_ref=dst, send_sem=send_sem, recv_sem=recv_sem, device_id=device, device_id_type=MESH).start()

    def waiter(ref, send_sem, recv_sem):
        return pltpu.make_async_remote_copy(
            src_ref=ref, dst_ref=ref, send_sem=send_sem, recv_sem=recv_sem, device_id=sibling, device_id_type=MESH)

    def drain(ref, sem):
        waiter(ref, out_sem.at[0], sem).wait_recv()

    def drain_sent(ref, sem):
        waiter(ref, sem, in_sem.at[0]).wait_send()

    buffers = {"L": fl, "A": fa, "B": fb}

    def slot_ref(kind, o, d):
        return buffers[kind].at[pl.ds(INDEX[o, d] * R, R), :]

    def sem_of(kind, o, d):
        return in_sem.at[KINDS.index(kind) * 9 + o * 5 + abs(d) - 1]

    def forward(kind, o, d):
        for direction, steps in routes(kind, o, d):
            target = (1 - o, d) if steps == 0 else (o, wrap(d - direction * steps))
            send(slot_ref(kind, o, d), slot_ref(kind, *target), out_sem.at[KINDS.index(kind)], sem_of(kind, *target),
                 hop(direction, steps))

    def take(kind, o, d):
        pair = (d, -d) if 0 < d < 4 else (d,)
        drain(buffers[kind].at[pl.ds(INDEX[o, d] * R, len(pair) * R), :], sem_of(kind, o, d))
        for each in pair:
            forward(kind, o, each)

    loads[0].wait()
    own_rows(lst, 0, KL, fl)
    pl.semaphore_wait(barrier, len(greeted))
    forward("L", 0, 0)
    loads[1].wait()
    for kind, (left, right) in COLUMNS.items():
        own_rows(rst, left, right - left, buffers[kind])
        forward(kind, 0, 0)

    loads[2].wait()
    loads[3].wait()
    hi, lo = split(turned(ob[...], g[...]))
    rgh[...] = hi
    rgl[...] = lo
    loads[4].wait()
    loads[5].wait()
    for c in range(7):
        columns = slice(c * BA, (c + 1) * BA)
        hi, lo = split(turned(ib[c], h[:, columns]))
        rah[columns, :] = hi
        ral[columns, :] = lo

    my_half = pl.multiple_of(core * 128, 128)
    its_half = pl.multiple_of((1 - core) * 128, 128)
    sent = [0, 0, 0, 0]

    def piece(b, n):
        first, last, _ = BATCHES[b]
        size = (last - first) * R // 16
        return pl.ds(pl.multiple_of(first * R + n * size, size), size)

    def send_mp(b, stage, src, dst, device):
        sent[stage] += src.shape[0]
        send(src, dst, mp_out.at[stage], mp_in.at[b, stage], device)

    def others(b):
        if BATCHES[b][2]:
            return [(chip_at(*p), peer(*p, 0)) for p in CHIPS]
        return [(chip_at(dy, a) * 2 + (1 - core if e else core), peer(dy, a, e)) for dy, a, e in PEERS]

    def size_of(b):
        return (BATCHES[b][1] - BATCHES[b][0]) * R // 16

    def coef(b):
        first, last, staged = BATCHES[b]
        x = fl[first * R:last * R, :]
        part[first * R:last * R, :] = mm(x, rgh[...]) + mm(x, rgl[...])
        if staged:
            send_mp(b, 0, part.at[pl.ds(first * R + its_half, 128)], ain.at[b], sibling)
        else:
            for k, (n, device) in enumerate(others(b)):
                send_mp(b, 1, part.at[piece(b, n)], bin_.at[b, pl.ds(k * size_of(b), size_of(b))], device)

    def core_sum(b):
        drain(ain.at[b], mp_in.at[b, 0])
        summed[b] = part[pl.ds(BATCHES[b][0] * R + my_half, 128)] + ain[b]
        for k, (n, device) in enumerate(others(b)):
            send_mp(b, 1, summed.at[b, pl.ds(pl.multiple_of(n * 16, 16), 16)], bin_.at[b, pl.ds(k * 16, 16)], device)

    def reduce(b):
        staged, size = BATCHES[b][2], size_of(b)
        n = 7 if staged else 15
        drain(bin_.at[b, pl.ds(0, n * size)], mp_in.at[b, 1])
        total = summed[b, pl.ds(pl.multiple_of(chip * 16, 16), 16)] if staged else part[piece(b, mp), :]
        for k in range(n):
            total = total + bin_[b, k * size:(k + 1) * size]
        half = my_half if staged else 0
        full[b, pl.ds(half, size)] = total
        for k, (_, device) in enumerate(others(b)):
            at = (lambda dy, a: dy * 2 + a)(*CHIPS[k]) if staged else (lambda dy, a, e: dy * 4 + a * 2 + e)(*PEERS[k])
            send_mp(b, 2, full.at[b, pl.ds(half, size)], full.at[b, pl.ds(half + at * size, size)], device)

    def whole(b):
        staged, size = BATCHES[b][2], size_of(b)
        half, n = (my_half, 7) if staged else (0, 15)
        drain(full.at[b, pl.ds(half + size, n * size)], mp_in.at[b, 2])
        if staged:
            rows = pl.ds(my_half, 128)
            send_mp(b, 3, full.at[b, rows], full.at[b, rows], sibling)

    def halves(b):
        drain(full.at[b, pl.ds(its_half, 128)], mp_in.at[b, 3])

    def project(first, last):
        r = slice(first * R, last * R)
        total = jnp.zeros(((last - first) * R, TOK), F32)
        for kind, (left, right) in COLUMNS.items():
            x = buffers[kind][r, :]
            total = total + (mm(x, rah[left:right, :]) + mm(x, ral[left:right, :]))
        proj[r, :] = total

    steps = {"coef": coef, "core": core_sum, "reduce": reduce, "whole": whole, "halves": halves, "proj": project}
    for step in ORDER:
        if step[0] in buffers:
            take(*step)
        else:
            steps[step[0]](*step[1:])

    slot_sums = []
    for b, (first, last, staged) in enumerate(BATCHES):
        size = size_of(b)
        per = R // size
        for i in range(last - first):
            total = jnp.zeros((size, TOK), F32)
            for n in range(i * per, (i + 1) * per):
                at = (n // 8) * 128 + chip_place(n % 8) * 16 if staged else place(n) * size
                total = total + (full[b, pl.ds(pl.multiple_of(at, size), size)]
                                 * proj[first * R + n * size:first * R + (n + 1) * size, :])
            slot_sums.append(jnp.sum(total, axis=0, keepdims=True))
    per_slot = jnp.concatenate(slot_sums, axis=0)
    table = pick[...]
    first = jnp.sum(jnp.sum(per_slot[:, :LEN], axis=1, keepdims=True) * table, axis=0, keepdims=True)
    second = jnp.sum(jnp.sum(per_slot[:, LEN:], axis=1, keepdims=True) * table, axis=0, keepdims=True)
    sub = lax.broadcasted_iota(jnp.int32, (8, 128), 0)
    tin[0] = jnp.where(sub == 0, first, jnp.where(sub == 1, second, jnp.float32(0)))
    for dy, a, e in PEERS:
        send(tin.at[0], tin.at[dy * 4 + a * 2 + e], mp_out.at[4], mp_in.at[0, 4], peer(dy, a, e))
    for kind, buffer in enumerate(buffers.values()):
        drain_sent(buffer.at[pl.ds(0, 15 * R)], out_sem.at[kind])
    for stage in range(4):
        if sent[stage]:
            drain_sent(part.at[pl.ds(0, sent[stage])], mp_out.at[stage])
    drain_sent(tin.at[pl.ds(0, 15)], mp_out.at[4])
    drain(tin.at[pl.ds(1, 15)], mp_in.at[0, 4])
    total = tin[place(0)]
    for i in range(1, 16):
        total = total + tin[place(i)]
    out[...] = total[:2, :NQ] * jnp.float32(1.0 / LEN)


def on_device(out_grads, hidden_acts, out_basis, in_basis, left_store, right_store, owners):
    n_batches = len(BATCHES)
    dma = pltpu.SemaphoreType.DMA
    return pl.pallas_call(
        kernel,
        out_shape=jax.ShapeDtypeStruct((2, NQ), F32),
        in_specs=[pl.BlockSpec(memory_space=pltpu.SMEM)] + [pl.BlockSpec(memory_space=pltpu.HBM)] * 6,
        out_specs=pl.BlockSpec(memory_space=pltpu.VMEM),
        scratch_shapes=[
            pltpu.VMEM((NQ * R, KL), BF16),
            pltpu.VMEM((NQ * R, KR), BF16),
            pltpu.VMEM((TOK, KL), BF16),
            pltpu.VMEM((TOK, KR), BF16),
            pltpu.VMEM((KL, KL), BF16),
            pltpu.VMEM((7, BA, BA), BF16),
            pltpu.VMEM((NQ * R, KL), BF16),
            *(pltpu.VMEM((NQ * R, right - left), BF16) for left, right in COLUMNS.values()),
            pltpu.VMEM((KL, TOK), BF16),
            pltpu.VMEM((KL, TOK), BF16),
            pltpu.VMEM((KR, TOK), BF16),
            pltpu.VMEM((KR, TOK), BF16),
            pltpu.VMEM((NQ, 128), F32),
            pltpu.VMEM((NQ * R, TOK), F32),
            pltpu.VMEM((n_batches, 128, TOK), F32),
            pltpu.VMEM((n_batches, 128, TOK), F32),
            pltpu.VMEM((n_batches, 120, TOK), F32),
            pltpu.VMEM((n_batches, NQ * R, TOK), F32),
            pltpu.VMEM((NQ * R, TOK), F32),
            pltpu.VMEM((16, 8, 128), F32),
            dma((6,)), dma((len(KINDS),)), dma((9 * len(KINDS),)), dma((5,)), dma((n_batches, 5)),
        ],
        compiler_params=pltpu.CompilerParams(
            collective_id=0, has_side_effects=True, vmem_limit_bytes=62 * 2 ** 20),
    )(owners, out_grads, hidden_acts, out_basis, in_basis, left_store, right_store)


def solution(mesh):
    in_specs = (
        P("dp", None),
        P("dp", "mp"),
        P("mp", None, None),
        P("mp", None, None),
        P("dp", None, "mp"),
        P("dp", None, "mp"),
        P(),
    )
    return jax.shard_map(on_device, mesh=mesh, in_specs=in_specs, out_specs=P("dp", None), check_vma=False)
```

```python
import functools

import jax
import jax.numpy as jnp
from jax import lax
from jax.experimental import pallas as pl
from jax.experimental.pallas import tpu as pltpu
from jax.sharding import PartitionSpec as P

NQ = 16
R = 32
LEN = 128
TOK = 256
KL = 512
KR = 1792
BA = 256
KINDS = "LAB"
MESH = pl.DeviceIdType.MESH
F32 = jnp.float32
BF16 = jnp.bfloat16

SLOTS = (
    (0, 0), (0, 1), (0, -1), (0, 2), (0, -2), (0, 3), (0, -3), (0, 4),
    (1, 0), (1, 1), (1, -1), (1, 2), (1, -2), (1, 3), (1, -3), (1, 4),
)
INDEX = {slot: i for i, slot in enumerate(SLOTS)}
BATCHES = ((0, 8, True), (8, 12, False), (12, 16, False))
COLUMNS = {"A": (0, 1024), "B": (1024, 1792)}
LEFT_ROUTES = {
    (0, 0): ((0, 0), (1, 1), (-1, 1), (1, 2), (-1, 2),),
    (0, 1): ((0, 0),),
    (0, -1): ((0, 0),),
    (0, 2): ((-1, 1), (0, 0),),
    (0, -2): ((1, 1), (1, 2), (0, 0),),
    (1, 2): ((-1, 1), (-1, 2),),
    (1, -2): ((1, 1),),
}
CROSS = {"A": (0, 1, -1, 4), "B": (0, 1, -1, 2, -2)}
LAST_OWN = {"A": 1, "B": -1}
LAST_OTHER = {"A": 1, "B": -1}

ORDER = (
    ("L", 0, 1), ("L", 1, 0), ("L", 0, 2), ("A", 1, 0), ("A", 0, 1), ("B", 1, 0), ("B", 0, 1), ("L", 0, 3),
    ("L", 1, 1), ("L", 0, 4), ("coef", 0), ("L", 1, 2), ("coef", 1), ("A", 0, 2), ("core", 0), ("B", 0, 2),
    ("proj", 0, 4), ("A", 1, 1), ("L", 1, 3), ("L", 1, 4), ("coef", 2), ("A", 0, 3), ("B", 1, 1), ("reduce", 1),
    ("B", 0, 3), ("reduce", 0), ("B", 1, 2), ("A", 1, 2), ("proj", 8, 12), ("A", 0, 4), ("reduce", 2), ("B", 0, 4),
    ("proj", 4, 8), ("B", 1, 3), ("whole", 1), ("A", 1, 3), ("whole", 0), ("A", 1, 4), ("B", 1, 4), ("proj", 12, 16),
    ("halves", 0), ("whole", 2),
)


def wrap(d):
    return (d + 3) % 8 - 3


def routes(kind, o, d):
    if kind == "L":
        return LEFT_ROUTES.get((o, d), ())
    out = []
    if o == 0:
        if -2 <= d <= 0 or (d == -3 and LAST_OWN[kind] == 1):
            out.append((1, 1))
        if 0 <= d <= 2 or (d == 3 and LAST_OWN[kind] == -1):
            out.append((-1, 1))
        if d in CROSS[kind]:
            out.append((0, 0))
    else:
        if d <= 0:
            t = wrap(d - 1)
            if t not in CROSS[kind] and (t != 4 or LAST_OTHER[kind] == 1):
                out.append((1, 1))
        if 0 <= d < 4:
            t = d + 1
            if t not in CROSS[kind] and (t != 4 or LAST_OTHER[kind] == -1):
                out.append((-1, 1))
    return out


CHIPS = tuple((dy, a) for dy in (2, 1, 3, 0) for a in (1, 0) if (dy, a) != (0, 0))
PEERS = tuple((dy, a, e) for dy in (2, 1, 3, 0) for a in (1, 0) for e in (1, 0) if (dy, a, e) != (0, 0, 0))


def split(x):
    hi = x.astype(BF16)
    return hi, (x - hi.astype(F32)).astype(BF16)


def turned(basis, rows):
    return lax.dot_general(basis, rows, (((0,), (1,)), ((), ())), preferred_element_type=F32)


def mm(a, b):
    return jnp.dot(a, b, preferred_element_type=F32)


def kernel(owners, grads, acts, out_basis, in_basis, left_store, right_store, out,
           lst, rst, g, h, ob, ib, fl, fa, fb, rgh, rgl, rah, ral, pick,
           part, ain, summed, bin_, full, proj, tin,
           load_sem, out_sem, in_sem, mp_out, mp_in):
    dp, mp = lax.axis_index("dp"), lax.axis_index("mp")
    xh, z = dp // 8, lax.rem(dp, 8)
    core = lax.rem(mp, 2)
    chip = mp // 2
    y, xl = chip // 2, lax.rem(chip, 2)

    def hop(direction, steps):
        if steps == 0:
            return ((1 - xh) * 8 + z, mp)
        return (xh * 8 + lax.rem(z + 8 + direction * steps, 8), mp)

    def chip_at(dy, a):
        return lax.rem(y + dy, 4) * 2 + (1 - xl if a else xl)

    def peer(dy, a, e):
        return (dp, chip_at(dy, a) * 2 + (1 - core if e else core))

    sibling = peer(0, 0, 1)

    def steps_from(chip_index):
        return lax.rem(y + 4 - chip_index // 2, 4), lax.rem(xl + chip_index, 2)

    def chip_place(n):
        dy, a = steps_from(n)
        return dy * 2 + a

    def place(n):
        return chip_place(n // 2) * 2 + lax.rem(core + n, 2)

    barrier = pltpu.get_barrier_semaphore()
    greeted = [hop(1, 1), hop(-1, 1), hop(-1, 2), hop(1, 2), hop(0, 0)] + [peer(*p) for p in PEERS]
    for device in greeted:
        pl.semaphore_signal(barrier, inc=1, device_id=device, device_id_type=MESH)

    loads = [
        pltpu.make_async_copy(left_store.at[0], lst, load_sem.at[0]),
        pltpu.make_async_copy(right_store.at[0], rst, load_sem.at[1]),
        pltpu.make_async_copy(grads.at[:, pl.ds(pl.multiple_of(mp * KL, KL), KL)], g, load_sem.at[2]),
        pltpu.make_async_copy(out_basis.at[0], ob, load_sem.at[3]),
        pltpu.make_async_copy(acts, h, load_sem.at[4]),
        pltpu.make_async_copy(in_basis, ib, load_sem.at[5]),
    ]
    for copy in loads:
        copy.start()

    row = lax.broadcasted_iota(jnp.int32, (NQ, 128), 0)
    lane = lax.broadcasted_iota(jnp.int32, (NQ, 128), 1)
    group = jnp.zeros((NQ, 128), jnp.int32)
    for i, (o, d) in enumerate(SLOTS):
        ring = 1 - xh if o else xh
        group = jnp.where(row == i, ring * 8 + lax.rem(z + 8 + d, 8), group)
    table = jnp.zeros((NQ, 128), F32)
    for q in range(NQ):
        table = jnp.where((lane == q) & (group == owners[q]), jnp.float32(1), table)
    pick[...] = table

    chosen = []
    for q in range(NQ):
        owned = jnp.full((R, 128), owners[q], jnp.int32) == dp
        chosen.append(jnp.where(owned, jnp.float32(1), jnp.float32(0)).astype(BF16))

    def own_rows(store, first, width, dest):
        for left in range(0, width, 128):
            columns = slice(first + left, first + left + 128)
            total = chosen[0] * store[0:R, columns]
            for q in range(1, NQ):
                total = total + chosen[q] * store[q * R:(q + 1) * R, columns]
            dest[0:R, left:left + 128] = total

    def send(src, dst, send_sem, recv_sem, device):
        pltpu.make_async_remote_copy(
            src_ref=src, dst_ref=dst, send_sem=send_sem, recv_sem=recv_sem, device_id=device, device_id_type=MESH).start()

    def waiter(ref, send_sem, recv_sem):
        return pltpu.make_async_remote_copy(
            src_ref=ref, dst_ref=ref, send_sem=send_sem, recv_sem=recv_sem, device_id=sibling, device_id_type=MESH)

    def drain(ref, sem):
        waiter(ref, out_sem.at[0], sem).wait_recv()

    def drain_sent(ref, sem):
        waiter(ref, sem, in_sem.at[0]).wait_send()

    buffers = {"L": fl, "A": fa, "B": fb}

    def slot_ref(kind, o, d):
        return buffers[kind].at[pl.ds(INDEX[o, d] * R, R), :]

    def sem_of(kind, o, d):
        return in_sem.at[KINDS.index(kind) * 9 + o * 5 + abs(d) - 1]

    def forward(kind, o, d):
        for direction, steps in routes(kind, o, d):
            target = (1 - o, d) if steps == 0 else (o, wrap(d - direction * steps))
            send(slot_ref(kind, o, d), slot_ref(kind, *target), out_sem.at[KINDS.index(kind)], sem_of(kind, *target),
                 hop(direction, steps))

    def take(kind, o, d):
        pair = (d, -d) if 0 < d < 4 else (d,)
        drain(buffers[kind].at[pl.ds(INDEX[o, d] * R, len(pair) * R), :], sem_of(kind, o, d))
        for each in pair:
            forward(kind, o, each)

    loads[0].wait()
    own_rows(lst, 0, KL, fl)
    pl.semaphore_wait(barrier, len(greeted))
    forward("L", 0, 0)
    loads[1].wait()
    for kind, (left, right) in COLUMNS.items():
        own_rows(rst, left, right - left, buffers[kind])
        forward(kind, 0, 0)

    loads[2].wait()
    loads[3].wait()
    hi, lo = split(turned(ob[...], g[...]))
    rgh[...] = hi
    rgl[...] = lo
    loads[4].wait()
    loads[5].wait()
    for c in range(7):
        columns = slice(c * BA, (c + 1) * BA)
        hi, lo = split(turned(ib[c], h[:, columns]))
        rah[columns, :] = hi
        ral[columns, :] = lo

    my_half = pl.multiple_of(core * 128, 128)
    its_half = pl.multiple_of((1 - core) * 128, 128)
    sent = [0, 0, 0, 0]

    def piece(b, n):
        first, last, _ = BATCHES[b]
        size = (last - first) * R // 16
        return pl.ds(pl.multiple_of(first * R + n * size, size), size)

    def send_mp(b, stage, src, dst, device):
        sent[stage] += src.shape[0]
        send(src, dst, mp_out.at[stage], mp_in.at[b, stage], device)

    def others(b):
        if BATCHES[b][2]:
            return [(chip_at(*p), peer(*p, 0)) for p in CHIPS]
        return [(chip_at(dy, a) * 2 + (1 - core if e else core), peer(dy, a, e)) for dy, a, e in PEERS]

    def size_of(b):
        return (BATCHES[b][1] - BATCHES[b][0]) * R // 16

    def coef(b):
        first, last, staged = BATCHES[b]
        x = fl[first * R:last * R, :]
        part[first * R:last * R, :] = mm(x, rgh[...]) + mm(x, rgl[...])
        if staged:
            send_mp(b, 0, part.at[pl.ds(first * R + its_half, 128)], ain.at[b], sibling)
        else:
            for k, (n, device) in enumerate(others(b)):
                send_mp(b, 1, part.at[piece(b, n)], bin_.at[b, pl.ds(k * size_of(b), size_of(b))], device)

    def core_sum(b):
        drain(ain.at[b], mp_in.at[b, 0])
        summed[b] = part[pl.ds(BATCHES[b][0] * R + my_half, 128)] + ain[b]
        for k, (n, device) in enumerate(others(b)):
            send_mp(b, 1, summed.at[b, pl.ds(pl.multiple_of(n * 16, 16), 16)], bin_.at[b, pl.ds(k * 16, 16)], device)

    def reduce(b):
        staged, size = BATCHES[b][2], size_of(b)
        n = 7 if staged else 15
        drain(bin_.at[b, pl.ds(0, n * size)], mp_in.at[b, 1])
        total = summed[b, pl.ds(pl.multiple_of(chip * 16, 16), 16)] if staged else part[piece(b, mp), :]
        for k in range(n):
            total = total + bin_[b, k * size:(k + 1) * size]
        half = my_half if staged else 0
        full[b, pl.ds(half, size)] = total
        for k, (_, device) in enumerate(others(b)):
            at = (lambda dy, a: dy * 2 + a)(*CHIPS[k]) if staged else (lambda dy, a, e: dy * 4 + a * 2 + e)(*PEERS[k])
            send_mp(b, 2, full.at[b, pl.ds(half, size)], full.at[b, pl.ds(half + at * size, size)], device)

    def whole(b):
        staged, size = BATCHES[b][2], size_of(b)
        half, n = (my_half, 7) if staged else (0, 15)
        drain(full.at[b, pl.ds(half + size, n * size)], mp_in.at[b, 2])
        if staged:
            rows = pl.ds(my_half, 128)
            send_mp(b, 3, full.at[b, rows], full.at[b, rows], sibling)

    def halves(b):
        drain(full.at[b, pl.ds(its_half, 128)], mp_in.at[b, 3])

    def project(first, last):
        r = slice(first * R, last * R)
        total = jnp.zeros(((last - first) * R, TOK), F32)
        for kind, (left, right) in COLUMNS.items():
            x = buffers[kind][r, :]
            total = total + (mm(x, rah[left:right, :]) + mm(x, ral[left:right, :]))
        proj[r, :] = total

    steps = {"coef": coef, "core": core_sum, "reduce": reduce, "whole": whole, "halves": halves, "proj": project}
    done = set()
    slot_sums = {}

    def multiply(b):
        first, last, staged = BATCHES[b]
        size = size_of(b)
        per = R // size
        for i in range(last - first):
            total = jnp.zeros((size, TOK), F32)
            for n in range(i * per, (i + 1) * per):
                at = (n // 8) * 128 + chip_place(n % 8) * 16 if staged else place(n) * size
                total = total + (full[b, pl.ds(pl.multiple_of(at, size), size)]
                                 * proj[first * R + n * size:first * R + (n + 1) * size, :])
            slot_sums[first + i] = jnp.sum(total, axis=0, keepdims=True)

    for step in ORDER:
        if step[0] in buffers:
            take(*step)
        else:
            steps[step[0]](*step[1:])
        done.add(step)
        for b, (first, last, staged) in enumerate(BATCHES):
            known = ("halves" if staged else "whole", b) in done
            contracted = {i for e in done if e[0] == "proj" for i in range(e[1], e[2])}
            if known and first not in slot_sums and contracted.issuperset(range(first, last)):
                multiply(b)

    per_slot = jnp.concatenate([slot_sums[i] for i in range(NQ)], axis=0)
    table = pick[...]
    first = jnp.sum(jnp.sum(per_slot[:, :LEN], axis=1, keepdims=True) * table, axis=0, keepdims=True)
    second = jnp.sum(jnp.sum(per_slot[:, LEN:], axis=1, keepdims=True) * table, axis=0, keepdims=True)
    sub = lax.broadcasted_iota(jnp.int32, (8, 128), 0)
    tin[0] = jnp.where(sub == 0, first, jnp.where(sub == 1, second, jnp.float32(0)))
    for dy, a, e in PEERS:
        send(tin.at[0], tin.at[dy * 4 + a * 2 + e], mp_out.at[4], mp_in.at[0, 4], peer(dy, a, e))
    for kind, buffer in enumerate(buffers.values()):
        drain_sent(buffer.at[pl.ds(0, 15 * R)], out_sem.at[kind])
    for stage in range(4):
        if sent[stage]:
            drain_sent(part.at[pl.ds(0, sent[stage])], mp_out.at[stage])
    drain_sent(tin.at[pl.ds(0, 15)], mp_out.at[4])
    drain(tin.at[pl.ds(1, 15)], mp_in.at[0, 4])
    total = tin[place(0)]
    for i in range(1, 16):
        total = total + tin[place(i)]
    out[...] = total[:2, :NQ] * jnp.float32(1.0 / LEN)


def on_device(out_grads, hidden_acts, out_basis, in_basis, left_store, right_store, owners):
    n_batches = len(BATCHES)
    dma = pltpu.SemaphoreType.DMA
    return pl.pallas_call(
        kernel,
        out_shape=jax.ShapeDtypeStruct((2, NQ), F32),
        in_specs=[pl.BlockSpec(memory_space=pltpu.SMEM)] + [pl.BlockSpec(memory_space=pltpu.HBM)] * 6,
        out_specs=pl.BlockSpec(memory_space=pltpu.VMEM),
        scratch_shapes=[
            pltpu.VMEM((NQ * R, KL), BF16),
            pltpu.VMEM((NQ * R, KR), BF16),
            pltpu.VMEM((TOK, KL), BF16),
            pltpu.VMEM((TOK, KR), BF16),
            pltpu.VMEM((KL, KL), BF16),
            pltpu.VMEM((7, BA, BA), BF16),
            pltpu.VMEM((NQ * R, KL), BF16),
            *(pltpu.VMEM((NQ * R, right - left), BF16) for left, right in COLUMNS.values()),
            pltpu.VMEM((KL, TOK), BF16),
            pltpu.VMEM((KL, TOK), BF16),
            pltpu.VMEM((KR, TOK), BF16),
            pltpu.VMEM((KR, TOK), BF16),
            pltpu.VMEM((NQ, 128), F32),
            pltpu.VMEM((NQ * R, TOK), F32),
            pltpu.VMEM((n_batches, 128, TOK), F32),
            pltpu.VMEM((n_batches, 128, TOK), F32),
            pltpu.VMEM((n_batches, 120, TOK), F32),
            pltpu.VMEM((n_batches, NQ * R, TOK), F32),
            pltpu.VMEM((NQ * R, TOK), F32),
            pltpu.VMEM((16, 8, 128), F32),
            dma((6,)), dma((len(KINDS),)), dma((9 * len(KINDS),)), dma((5,)), dma((n_batches, 5)),
        ],
        compiler_params=pltpu.CompilerParams(
            collective_id=0, has_side_effects=True, vmem_limit_bytes=62 * 2 ** 20),
    )(owners, out_grads, hidden_acts, out_basis, in_basis, left_store, right_store)


def solution(mesh):
    in_specs = (
        P("dp", None),
        P("dp", "mp"),
        P("mp", None, None),
        P("mp", None, None),
        P("dp", None, "mp"),
        P("dp", None, "mp"),
        P(),
    )
    return jax.shard_map(on_device, mesh=mesh, in_specs=in_specs, out_specs=P("dp", None), check_vma=False)
```
